512 devices in a mesh: dp: 64 (over y, z), tensor: 8 (over x, core).
Axes of the slice: x: 4, y: 8, z: 8, core: 2. Of those that a mesh axis runs over, the one named last changes fastest.
Arguments:
- embeddings: bfloat16 [8192, 128, 128], P('dp', 'tensor'), may hold values from -1.1953125 to 1.1953125
- projection: bfloat16 [128, 4], replicated, may hold values from -0.5 to 0.5
- layer_norm_gain: float32 [512], replicated, may hold values from 0.5 to 1.5
- weight_in: bfloat16 [512, 8192], P(None, 'tensor'), may hold values from -0.25 to 0.25
- weight_out: bfloat16 [8192, 512], P('tensor'), may hold values from -0.0625 to 0.0625
- out_grad: bfloat16 [8192, 512], P('dp'), may hold values from -6 to 6
- left_start: float32 [64, 8192], P(None, 'tensor'), may hold values from -6 to 6
- right_start: float32 [64, 512], replicated, may hold values from -6 to 6
Outputs:
- emb_grad: bfloat16 [8192, 128, 128], P('dp', 'tensor')
- left_basis: float32 [64, 512], replicated
- left_update: float32 [64, 8192], P(None, 'tensor')
- right_basis: float32 [64, 8192], P(None, 'tensor')
- right_update: float32 [64, 512], replicated
The draws below stay inside these ranges and needn't reach their ends.
All inputs are finite; a program needn't handle non-finite values.
Results may differ from the reference program's by a relative error of at most 0.0089.
Values sent between devices are 32-bit elements; how exact they have to be, the bound alone decides.
A program may use at most 64 MiB of HBM per device.

```python
import jax
import jax.numpy as jnp
from jax import lax

E = 128
DE = 128
KF = 4
H = 8192
RANK = 64
EX_DEV = 128
IN = 512
OUT = 512
EXAMPLES = 8192
N_DP = 64


def block_scale(rng, dims, pieces, low, high):
    def one(position, blocks):
        draws = jax.random.uniform(jax.random.fold_in(jax.random.fold_in(rng, 6), position), (blocks,), jnp.float32, low / len(pieces), high / len(pieces))
        return jnp.repeat(jnp.exp(draws), dims[position] // blocks).reshape((-1,) + (1,) * (len(dims) - position - 1))

    factor_of = one(*pieces[0])
    for cut in pieces[1:]:
        factor_of = factor_of * one(*cut)
    return factor_of


def scatter_about(stream_key, dims, deviation, bound, split=(), dtype=jnp.bfloat16):
    level = block_scale(stream_key, dims, split, -0.22, 0.18) if split else 1.0
    array = jax.random.normal(stream_key, dims, jnp.float32) * deviation * level
    return jnp.minimum(jnp.maximum(array, -bound), bound).astype(dtype)


def setup_inputs(seed: int = 0) -> dict:
    splits = jax.random.split(jax.random.key(seed), 9)
    embeddings = scatter_about(splits[0], (EXAMPLES, DE, E), 0.2, 1.1953125, ((0, 64), (1, 8)))
    projection = scatter_about(splits[1], (E, KF), E ** -0.5, 0.5)
    layer_norm_gain = jnp.clip(1.0 + 0.1 * jax.random.normal(splits[2], (IN,), jnp.float32), 0.5, 1.5)
    weight_in = scatter_about(splits[3], (IN, H), IN ** -0.5, 0.25, ((1, 8),))
    weight_out = scatter_about(splits[4], (H, OUT), H ** -0.5, 0.0625, ((0, 8),))
    out_grad = scatter_about(splits[5], (EXAMPLES, OUT), 1.0, 6.0, ((0, 64),))
    left_start = scatter_about(splits[6], (RANK, H), 1.0, 6.0, ((1, 8),), jnp.float32)
    right_start = scatter_about(splits[7], (RANK, OUT), 1.0, 6.0, (), jnp.float32)
    return dict(embeddings=embeddings, projection=projection, layer_norm_gain=layer_norm_gain, weight_in=weight_in, weight_out=weight_out, out_grad=out_grad, left_start=left_start, right_start=right_start)


HIGH = lax.Precision.HIGHEST

def features_of(block, projection):
    values = block.astype(jnp.float32)
    inner = jnp.einsum('nde,ndf->nef', values, values, precision=HIGH)
    mixed = jnp.einsum('nef,fk->nek', inner, projection.astype(jnp.float32), precision=HIGH)
    return mixed.reshape(values.shape[0], -1)

def grad_of(pair, projection):
    block, d_feat = pair
    count = block.shape[0]
    d_blocks = d_feat.reshape(count, block.shape[2], -1)
    d_inner = jnp.einsum('nek,jk->nej', d_blocks, projection.astype(jnp.float32), precision=HIGH)
    sym = (d_inner + jnp.transpose(d_inner, (0, 2, 1))).astype(jnp.bfloat16)
    result = jnp.einsum('ndj,njm->ndm', block.astype(jnp.float32), sym.astype(jnp.float32), precision=HIGH)
    return result.astype(jnp.bfloat16)

def orthonormal(matrix):
    gram_matrix = jnp.dot(matrix, matrix.T, precision=HIGH)
    lower_factor = jnp.linalg.cholesky(gram_matrix)
    return lax.linalg.triangular_solve(lower_factor, matrix, left_side=True, lower=True)

def reference(embeddings, projection, layer_norm_gain, weight_in, weight_out, out_grad, left_start, right_start):
    blocks = embeddings.reshape(N_DP, EX_DEV, DE, E)
    features = lax.map(lambda block: features_of(block, projection), blocks).reshape(EXAMPLES, IN)
    center = lax.optimization_barrier(jnp.mean(features, axis=1, keepdims=True))
    centered_input = features - center
    inverse_deviation = lax.rsqrt(lax.optimization_barrier(jnp.mean(centered_input * centered_input, axis=1, keepdims=True)) + 1e-05)
    standardized_input = centered_input * inverse_deviation
    normalized_input = (standardized_input * layer_norm_gain).astype(jnp.bfloat16)
    pre = jnp.dot(normalized_input.astype(jnp.float32), weight_in.astype(jnp.float32), preferred_element_type=jnp.float32)
    sigma = jax.nn.sigmoid(pre)
    hidden = (pre * sigma).astype(jnp.bfloat16)
    d_hidden = jnp.dot(out_grad.astype(jnp.float32), weight_out.T.astype(jnp.float32), preferred_element_type=jnp.float32)
    d_pre = (d_hidden * sigma * (1.0 + pre * (1.0 - sigma))).astype(jnp.bfloat16)
    factor = 1.0 / jnp.sqrt(jnp.float32(EXAMPLES))
    grad_in = jnp.dot(normalized_input.T.astype(jnp.float32), d_pre.astype(jnp.float32), preferred_element_type=jnp.float32) * factor
    grad_out = jnp.dot(hidden.T.astype(jnp.float32), out_grad.astype(jnp.float32), preferred_element_type=jnp.float32) * factor
    d_normed = jnp.dot(d_pre.astype(jnp.float32), weight_in.T.astype(jnp.float32), preferred_element_type=jnp.float32)
    gradient_scaled = d_normed * layer_norm_gain
    feature_gradient = (gradient_scaled - lax.optimization_barrier(jnp.mean(gradient_scaled, axis=1, keepdims=True)) - standardized_input * lax.optimization_barrier(jnp.mean(gradient_scaled * standardized_input, axis=1, keepdims=True))) * inverse_deviation
    d_blocks = feature_gradient.reshape(N_DP, EX_DEV, IN)
    emb_grad = lax.map(lambda pair: grad_of(pair, projection), (blocks, d_blocks)).reshape(EXAMPLES, DE, E)
    left_basis = orthonormal(jnp.dot(left_start, grad_in.T, precision=HIGH))
    left_update = jnp.dot(left_basis, grad_in, precision=HIGH)
    right_basis = orthonormal(jnp.dot(right_start, grad_out.T, precision=HIGH))
    right_update = jnp.dot(right_basis, grad_out, precision=HIGH)
    return (emb_grad, left_basis, left_update, right_basis, right_update)
```

```python
import functools
import math

import jax
import jax.numpy as jnp
from jax import lax
from jax.experimental import pallas as pl
from jax.experimental.pallas import tpu as pltpu
from jax.sharding import PartitionSpec as P

F32 = jnp.float32
BF16 = jnp.bfloat16
HIGH = lax.Precision.HIGHEST
MESH = pl.DeviceIdType.MESH
LANES = 128
KF = 4
GROUP = 16
AUG = 64

(FEAT, NORMED, DNORM, DFEAT, T_SUM, A1_0, A1_1, A2_0, A2_1, A3_0, A3_1, L1_0, L1_1, L2_0, L2_1, L3, GRAM,
 V_SUM, B1_0, B1_1, B2_0, B2_1, B3_0, B3_1, S1_0, S1_1, S2_0, S2_1, S3, STAGES) = range(30)


def dot(a, b):
    return jnp.dot(a, b, preferred_element_type=F32)


def dot_t(a, b):
    return lax.dot_general(a, b, (((1,), (1,)), ((), ())), preferred_element_type=F32)


def pieces(a, count=3):
    parts = []
    for _ in range(count):
        part = a.astype(BF16).astype(F32)
        parts.append(part)
        a = a - part
    return parts


def stacked(a):
    return jnp.concatenate(pieces(a), axis=0).astype(BF16)


def stacked_small(a):
    parts = pieces(a)
    return jnp.concatenate(parts + [jnp.zeros_like(a)], axis=0).astype(BF16)


def unstack(a, rows):
    return a[:rows] + (a[rows : 2 * rows] + a[2 * rows : 3 * rows])


def iota(shape, axis):
    return lax.broadcasted_iota(jnp.int32, shape, axis)


def kernel(
    nt, ny, nz, factor,
    x_hbm, proj_ref, gain_ref, win_hbm, wout_hbm, og_hbm, ls_hbm, rs_hbm,
    emb_hbm, lbasis_ref, lupd_ref, rbasis_ref, rupd_ref,
    x, win, wout, og, ls, rs,
    wp, perm, dhid, hid, dpre, ls3, og_r3, emb, pt,
    feat_send, feat_recv, norm, norm_bf, dn_send, dn_recv, dfeat,
    t_send, t_recv, big_send, big1, big2_send, big2, raw, upd,
    small_send, small1, small2_send, small2, lraw, rupd,
    gram_all, aug,
    local_sems, send_sems, recv_sems,
):
    rank, hidden = ls.shape
    rows = x.shape[0]
    examples = norm.shape[0]
    half = hidden // 2
    width = norm.shape[1]
    dp, t = lax.axis_index("dp"), lax.axis_index("tensor")
    y, z = dp // nz, dp % nz

    def peers(axis):
        if axis == "t":
            return t, [(p, (dp, p)) for p in ((t + i) % nt for i in range(1, nt))]
        if axis == "y":
            return y, [(p, (p * nz + z, t)) for p in ((y + i) % ny for i in range(1, ny))]
        return z, [(p, (y * nz + p, t)) for p in ((z + i) % nz for i in range(1, nz))]

    groups = {axis: peers(axis) for axis in "tyz"}

    barrier = pltpu.get_barrier_semaphore()
    for axis in "tyz":
        for _, device in groups[axis][1]:
            pl.semaphore_signal(barrier, inc=1, device_id=device, device_id_type=MESH)

    def remote(stage, i, axis, src, dst, sem, device):
        return pltpu.make_async_remote_copy(
            src_ref=src, dst_ref=dst, send_sem=send_sems.at[stage, i], recv_sem=recv_sems.at[stage, sem],
            device_id=device, device_id_type=MESH,
        )

    def send_one(stage, axis, i, src, dst):
        me, others = groups[axis]
        p, device = others[i]
        remote(stage, i, axis, src(p), dst(me), me, device).start()

    def send(stage, axis, src, dst):
        for i in range(len(groups[axis][1])):
            send_one(stage, axis, i, src, dst)

    sent = []

    def receive(stage, axis, src, dst):
        me, others = groups[axis]
        for i, (p, device) in enumerate(others):
            remote(stage, i, axis, dst(p), dst(p), p, device).wait_recv()
        sent.append((stage, axis, src))

    def drain():
        for stage, axis, src in sent:
            for i, (p, device) in enumerate(groups[axis][1]):
                remote(stage, i, axis, src(p), src(p), p, device).wait_send()
        sent.clear()

    loads = [
        pltpu.make_async_copy(a, b, local_sems.at[i])
        for i, (a, b) in enumerate(
            ((x_hbm, x), (win_hbm, win), (og_hbm, og), (wout_hbm, wout), (ls_hbm, ls), (rs_hbm, rs))
        )
    ]
    for load in loads:
        load.start()

    pick = (iota((KF * GROUP, KF), 0) // GROUP == iota((KF * GROUP, KF), 1)).astype(F32).astype(BF16)
    pt[...] = dot_t(pick, proj_ref[...]).astype(BF16)

    loads[0].wait()
    own = KF * GROUP
    y_t = dot_t(pt[...], x[...])
    block = GROUP * (rows // examples)
    keep = iota((own, rows), 0) % GROUP == (iota((own, rows), 1) // (rows // examples)) % GROUP
    y_t = jnp.where(keep, y_t, 0.0)
    y_hi, y_lo = pieces(y_t, 2)
    y_both = jnp.concatenate([y_hi, y_lo], axis=0).astype(BF16)
    for g in range(nt):
        both = dot(y_both[:, g * block : (g + 1) * block], x[g * block : (g + 1) * block, :])
        out = both[:own] + both[own:]
        for k in range(KF):
            feat_send[g, :, k * LANES : (k + 1) * LANES] = out[k * GROUP : (k + 1) * GROUP]
    pl.semaphore_wait(barrier, sum(len(groups[axis][1]) for axis in "tyz"))
    feat_src = lambda p: feat_send.at[p]
    feat_dst = lambda p: feat_recv.at[p]
    send(FEAT, "t", feat_src, feat_dst)
    feat_recv[t] = feat_send[t]

    column = iota((width, width), 1)
    row = iota((width, width), 0)
    perm[...] = (column == (row % LANES) * KF + row // LANES).astype(F32).astype(BF16)
    gain_rows = jnp.concatenate(pieces(gain_ref[...]) + [jnp.zeros((5, width), F32)], axis=0).astype(BF16)
    gain = dot_t(gain_rows, perm[...])
    gain = gain[0:1] + (gain[1:2] + gain[2:3])
    loads[1].wait()
    step = min(256, half)
    for c in range(0, hidden, step):
        wp[:, c : c + step] = dot(perm[...], win[:, c : c + step]).astype(BF16)
    loads[2].wait()
    loads[5].wait()
    og_r = unstack(dot_t(stacked(rs[...]), og[...]), rank) * factor
    og_r3[...] = stacked(og_r)
    loads[3].wait()
    for c in range(0, hidden, step):
        dhid[:, c : c + step] = dot_t(og[...], wout[c : c + step, :])
    loads[4].wait()
    ls3[...] = stacked(ls[...])

    receive(FEAT, "t", feat_src, feat_dst)
    features = feat_recv[0]
    for p in range(1, nt):
        features = features + feat_recv[p]
    centered = features - jnp.sum(features, axis=1, keepdims=True) * (1.0 / width)
    rstd = lax.rsqrt(jnp.sum(centered * centered, axis=1, keepdims=True) * (1.0 / width) + 1e-05)
    xhat = centered * rstd
    mine = pl.ds(pl.multiple_of(t * GROUP, GROUP), GROUP)
    norm[mine, :] = (xhat * gain).astype(BF16).astype(F32)
    norm_dst = lambda p: norm.at[pl.ds(pl.multiple_of(p * GROUP, GROUP), GROUP), :]
    norm_src = lambda p: norm.at[mine, :]
    send(NORMED, "t", norm_src, norm_dst)
    receive(NORMED, "t", norm_src, norm_dst)
    norm_bf[...] = norm[...].astype(BF16)

    for c in range(0, hidden, step):
        cols = slice(c, c + step)
        pre = dot(norm_bf[...], wp[:, cols])
        sigma = jax.nn.sigmoid(pre)
        hid[:, cols] = (pre * sigma).astype(BF16)
        dpre[:, cols] = (dhid[:, cols] * sigma * (1.0 + pre * (1.0 - sigma))).astype(BF16)

    def factor_sum(stage, value):
        t_send[int(stage == V_SUM)] = value
        src = lambda p: t_send.at[int(stage == V_SUM), pl.ds(pl.multiple_of(p * 8, 8), 8), :]
        dst = lambda p: t_recv.at[int(stage == V_SUM), p]
        send(stage, "t", src, dst)
        t_recv[int(stage == V_SUM), t] = t_send[int(stage == V_SUM), pl.ds(pl.multiple_of(t * 8, 8), 8), :]

        def finish():
            receive(stage, "t", src, dst)
            total = t_recv[int(stage == V_SUM), 0]
            for p in range(1, nt):
                total = total + t_recv[int(stage == V_SUM), p]
            return total

        return finish

    def eight(p):
        return pl.ds(pl.multiple_of(p * 8, 8), 8)

    def total_of(ref, count):
        total = ref[0]
        for p in range(1, count):
            total = total + ref[p]
        return total

    def big_first(r, h):
        stage, axis = ((A1_0, A1_1), (B1_0, B1_1))[r][h], "yz"[h]
        cols = pl.ds(h * half, half)
        src = lambda p: big_send.at[r, eight(p), cols]
        dst = lambda p: big1.at[r, h, p]
        send(stage, axis, src, dst)
        me = groups[axis][0]
        big1[r, h, me] = big_send[r, eight(me), h * half : (h + 1) * half]
        return lambda: receive(stage, axis, src, dst)

    def big_second(r, h):
        stage, axis = ((A2_0, A2_1), (B2_0, B2_1))[r][h], "zy"[h]
        value = total_of(big1.at[r, h], (ny, nz)[h])
        big2_send[r, h] = value
        me = groups[axis][0]
        src = lambda p: big2_send.at[r, h]
        dst = lambda p: big2.at[r, h, p]
        send(stage, axis, src, dst)
        big2[r, h, me] = value
        return lambda: receive(stage, axis, src, dst)

    def big_third(r, h, target):
        stage, axis = ((A3_0, A3_1), (B3_0, B3_1))[r][h], "yz"[h]
        value = total_of(big2.at[r, h], (nz, ny)[h])
        me = groups[axis][0]
        cols = pl.ds(h * half, half)
        target[eight(me), h * half : (h + 1) * half] = value
        src = lambda p: target.at[eight(me), cols]
        dst = lambda p: target.at[eight(p), cols]
        send(stage, axis, src, dst)
        return lambda: receive(stage, axis, src, dst)

    quarter = width // 2

    def small_first(r, h, value):
        stage, axis = ((L1_0, L1_1), (S1_0, S1_1))[r][h], "yz"[h]
        small_send[r, h] = value
        me = groups[axis][0]
        src = lambda p: small_send.at[r, h]
        dst = lambda p: small1.at[r, h, p]
        send(stage, axis, src, dst)
        small1[r, h, me] = value
        return lambda: receive(stage, axis, src, dst)

    def small_second(r, h):
        stage, axis = ((L2_0, L2_1), (S2_0, S2_1))[r][h], "zy"[h]
        value = total_of(small1.at[r, h], (ny, nz)[h])
        small2_send[r, h] = value
        me = groups[axis][0]
        src = lambda p: small2_send.at[r, h]
        dst = lambda p: small2.at[r, h, p]
        send(stage, axis, src, dst)
        small2[r, h, me] = value
        return lambda: receive(stage, axis, src, dst)

    def small_third(r, target):
        stage = (L3, S3)[r]
        for h in range(2):
            target[eight(t), h * quarter : (h + 1) * quarter] = total_of(small2.at[r, h], (nz, ny)[h])
        src = lambda p: target.at[eight(t), :]
        dst = lambda p: target.at[eight(p), :]
        send(stage, "t", src, dst)
        return lambda: receive(stage, "t", src, dst)

    t_done = factor_sum(T_SUM, unstack(dot_t(ls3[...], dpre[...]), rank) * factor)
    a1 = []
    for h in range(2):
        big_send[0, :, h * half : (h + 1) * half] = unstack(dot(og_r3[...], hid[:, h * half : (h + 1) * half]), rank)
        a1.append(big_first(0, h))
    left = unstack(dot(stacked_small(t_done()), norm_bf[...]), 8)
    l1 = [small_first(0, h, left[:, h * quarter : (h + 1) * quarter]) for h in range(2)]

    d_partial = dot_t(dpre[...], wp[...])
    for g in range(nt):
        dn_send[g] = d_partial[g * GROUP : (g + 1) * GROUP]
    dn_src = lambda p: dn_send.at[p]
    dn_dst = lambda p: dn_recv.at[p]
    send(DNORM, "t", dn_src, dn_dst)
    dn_recv[t] = dn_send[t]

    a2 = []
    for h in range(2):
        a1[h]()
        a2.append(big_second(0, h))
    l2 = []
    for h in range(2):
        l1[h]()
        l2.append(small_second(0, h))
    a3 = []
    for h in range(2):
        a2[h]()
        a3.append(big_third(0, h, raw))
    for h in range(2):
        l2[h]()
    l3 = small_third(0, lraw)

    receive(DNORM, "t", dn_src, dn_dst)
    scaled = total_of(dn_recv, nt) * gain
    mean = jnp.sum(scaled, axis=1, keepdims=True) * (1.0 / width)
    slope = jnp.sum(scaled * xhat, axis=1, keepdims=True) * (1.0 / width)
    dfeat[mine, :] = (scaled - mean - xhat * slope) * rstd
    df_src = lambda p: dfeat.at[mine, :]
    df_dst = lambda p: dfeat.at[pl.ds(pl.multiple_of(p * GROUP, GROUP), GROUP), :]
    send(DFEAT, "t", df_src, df_dst)

    for h in range(2):
        a3[h]()
    v_done = factor_sum(V_SUM, unstack(dot_t(stacked(raw[...]), hid[...]), rank) * factor)
    gram = lax.dot_general(raw[...], raw[...], (((1,), (1,)), ((), ())), precision=HIGH, preferred_element_type=F32)
    gram_all[t] = jnp.concatenate([gram, jnp.zeros((rank, LANES - rank), F32)], axis=1)
    gram_src = lambda p: gram_all.at[t]
    gram_dst = lambda p: gram_all.at[p]
    send(GRAM, "t", gram_src, gram_dst)

    l3()
    u = unstack(dot_t(stacked(lraw[...]), norm_bf[...]), rank) * factor
    u3 = stacked(u)
    b1 = []
    for h in range(2):
        big_send[1, :, h * half : (h + 1) * half] = unstack(dot(u3, dpre[:, h * half : (h + 1) * half]), rank)
        b1.append(big_first(1, h))
    right = unstack(dot(stacked_small(v_done()), og[...]), 8)
    s1 = [small_first(1, h, right[:, h * quarter : (h + 1) * quarter]) for h in range(2)]

    receive(DFEAT, "t", df_src, df_dst)
    pt_all = jnp.concatenate([pt[...]] * 4, axis=0)
    pt_two = jnp.concatenate([pt[...]] * 2, axis=0)
    same = iota((block, 2 * own), 0) // (rows // examples) == iota((block, 2 * own), 1) % GROUP

    def grad_group(g):
        part = pl.ds(pl.multiple_of(g * block, block), block)
        d = dfeat[pl.ds(pl.multiple_of(g * GROUP, GROUP), GROUP), :]
        d = jnp.concatenate([d[:, k * LANES : (k + 1) * LANES] for k in range(KF)], axis=0)
        d_two = jnp.concatenate(pieces(d, 2), axis=0).astype(BF16)
        xg = x[part, :]
        through = jnp.where(same, dot_t(xg, d_two), 0.0)
        mixed = jnp.where(same, dot_t(xg, pt_two), 0.0)
        through = jnp.concatenate(pieces(through, 2), axis=1).astype(BF16)
        mixed = jnp.concatenate(pieces(mixed, 2), axis=1).astype(BF16)
        d_all = jnp.concatenate([d_two, d_two], axis=0)
        emb[part, :] = (dot(through, pt_all) + dot(mixed, d_all)).astype(BF16)

    for g in range(nt):
        grad_group(g)
    store = pltpu.make_async_copy(emb, emb_hbm, local_sems.at[6])
    store.start()

    b2 = []
    for h in range(2):
        b1[h]()
        b2.append(big_second(1, h))
    s2 = []
    for h in range(2):
        s1[h]()
        s2.append(small_second(1, h))

    unit = (iota((rank, LANES), 1) - AUG == iota((rank, LANES), 0)).astype(F32)
    left_gram = lax.dot_general(lraw[...], lraw[...], (((1,), (1,)), ((), ())), precision=HIGH, preferred_element_type=F32)
    aug[0] = jnp.concatenate([left_gram, jnp.zeros((rank, LANES - rank), F32)], axis=1) + unit
    receive(GRAM, "t", gram_src, gram_dst)
    aug[1] = total_of(gram_all, nt) + unit

    lane = iota((rank, LANES), 1)
    sub = iota((rank, LANES), 0)

    def eliminate(k, carry):
        for m in range(2):
            a = aug[m]
            top = aug[m, pl.ds(k, 1), :]
            pivot = jnp.sum(jnp.where(lane[0:1] == k, top, 0.0), axis=1, keepdims=True)
            column = jnp.sum(jnp.where(lane == k, a, 0.0), axis=1, keepdims=True)
            column = jnp.where(sub[:, 0:1] > k, column, 0.0)
            aug[m] = a - column * (top / pivot)
        return carry

    lax.fori_loop(0, rank, eliminate, 0)

    b3 = []
    for h in range(2):
        b2[h]()
        b3.append(big_third(1, h, upd))
    for h in range(2):
        s2[h]()
    s3 = small_third(1, rupd)

    def inverse(m):
        a = aug[m]
        diagonal = jnp.sum(jnp.where(lane == sub, a, 0.0), axis=1, keepdims=True)
        return a[:, AUG : AUG + rank] * lax.rsqrt(diagonal)

    def high(a, b):
        return jnp.dot(a, b, precision=HIGH, preferred_element_type=F32)

    left_inv, right_inv = inverse(0), inverse(1)
    lbasis_ref[...] = unstack(dot(stacked(high(left_inv, lraw[...])), perm[...]), rank)
    rbasis_ref[...] = high(right_inv, raw[...])
    drain()
    for h in range(2):
        b3[h]()
    lupd_ref[...] = high(left_inv, upd[...])
    s3()
    rupd_ref[...] = high(right_inv, rupd[...])
    drain()
    store.wait()


def solution(mesh):
    nt = mesh.shape["tensor"]
    ny = nz = math.isqrt(mesh.shape["dp"])

    def on_device(embeddings, projection, gain, weight_in, weight_out, out_grad, left_start, right_start):
        examples, slice_width, emb_width = embeddings.shape
        rows = examples * slice_width
        width, hidden = weight_in.shape
        rank = left_start.shape[0]
        factor = 1.0 / math.sqrt(examples * ny * nz)
        half, quarter = hidden // 2, width // 2
        vmem = pl.BlockSpec(memory_space=pltpu.VMEM)
        hbm = pl.BlockSpec(memory_space=pl.ANY)
        n = max(ny, nz)
        out = pl.pallas_call(
            functools.partial(kernel, nt, ny, nz, factor),
            out_shape=(
                jax.ShapeDtypeStruct((rows, emb_width), BF16),
                jax.ShapeDtypeStruct((rank, width), F32),
                jax.ShapeDtypeStruct((rank, hidden), F32),
                jax.ShapeDtypeStruct((rank, hidden), F32),
                jax.ShapeDtypeStruct((rank, width), F32),
            ),
            in_specs=[hbm, vmem, vmem, hbm, hbm, hbm, hbm, hbm],
            out_specs=(hbm, vmem, vmem, vmem, vmem),
            scratch_shapes=[
                pltpu.VMEM((rows, emb_width), BF16),
                pltpu.VMEM((width, hidden), BF16),
                pltpu.VMEM(weight_out.shape, BF16),
                pltpu.VMEM(out_grad.shape, BF16),
                pltpu.VMEM((rank, hidden), F32),
                pltpu.VMEM(right_start.shape, F32),
                pltpu.VMEM((width, hidden), BF16),
                pltpu.VMEM((width, width), BF16),
                pltpu.VMEM((examples, hidden), F32),
                pltpu.VMEM((examples, hidden), BF16),
                pltpu.VMEM((examples, hidden), BF16),
                pltpu.VMEM((3 * rank, hidden), BF16),
                pltpu.VMEM((3 * rank, examples), BF16),
                pltpu.VMEM((rows, emb_width), BF16),
                pltpu.VMEM((KF * GROUP, emb_width), BF16),
                pltpu.VMEM((nt, GROUP, width), F32),
                pltpu.VMEM((nt, GROUP, width), F32),
                pltpu.VMEM((examples, width), F32),
                pltpu.VMEM((examples, width), BF16),
                pltpu.VMEM((nt, GROUP, width), F32),
                pltpu.VMEM((nt, GROUP, width), F32),
                pltpu.VMEM((examples, width), F32),
                pltpu.VMEM((2, rank, examples), F32),
                pltpu.VMEM((2, nt, 8, examples), F32),
                pltpu.VMEM((2, rank, hidden), F32),
                pltpu.VMEM((2, 2, n, 8, half), F32),
                pltpu.VMEM((2, 2, 8, half), F32),
                pltpu.VMEM((2, 2, n, 8, half), F32),
                pltpu.VMEM((rank, hidden), F32),
                pltpu.VMEM((rank, hidden), F32),
                pltpu.VMEM((2, 2, 8, quarter), F32),
                pltpu.VMEM((2, 2, n, 8, quarter), F32),
                pltpu.VMEM((2, 2, 8, quarter), F32),
                pltpu.VMEM((2, 2, n, 8, quarter), F32),
                pltpu.VMEM((rank, width), F32),
                pltpu.VMEM((rank, width), F32),
                pltpu.VMEM((nt, rank, LANES), F32),
                pltpu.VMEM((2, rank, LANES), F32),
                pltpu.SemaphoreType.DMA((7,)),
                pltpu.SemaphoreType.DMA((STAGES, max(n, nt))),
                pltpu.SemaphoreType.DMA((STAGES, max(n, nt))),
            ],
            compiler_params=pltpu.CompilerParams(
                collective_id=0, has_side_effects=True, vmem_limit_bytes=48 * 1024 * 1024
            ),
            name="fused_backward",
        )(
            embeddings.reshape(rows, emb_width), projection, gain.reshape(1, width),
            weight_in, weight_out, out_grad, left_start, right_start,
        )
        return (out[0].reshape(embeddings.shape), *out[1:])

    return jax.shard_map(
        on_device,
        mesh=mesh,
        in_specs=(
            P("dp", "tensor", None),
            P(),
            P(),
            P(None, "tensor"),
            P("tensor", None),
            P("dp", None),
            P(None, "tensor"),
            P(),
        ),
        out_specs=(P("dp", "tensor", None), P(), P(None, "tensor"), P(None, "tensor"), P()),
        check_vma=False,
    )
```

```python
import functools
import math

import jax
import jax.numpy as jnp
from jax import lax
from jax.experimental import pallas as pl
from jax.experimental.pallas import tpu as pltpu
from jax.sharding import PartitionSpec as P

F32 = jnp.float32
BF16 = jnp.bfloat16
HIGH = lax.Precision.HIGHEST
MESH = pl.DeviceIdType.MESH
LANES = 128
KF = 4
GROUP = 16
AUG = 64

(FEAT_C, FEAT, NORM_C, NORM_X, NORM_F, DNORM, DFEAT, T_SUM, A1_0, A1_1, A2_0, A2_1, A3_0, A3_1, L1_0, L1_1, L2_0, L2_1, L3, GRAM,
 V_SUM, B1_0, B1_1, B2_0, B2_1, B3_0, B3_1, S1_0, S1_1, S2_0, S2_1, S3, STAGES) = range(33)


def dot(a, b):
    return jnp.dot(a, b, preferred_element_type=F32)


def dot_t(a, b):
    return lax.dot_general(a, b, (((1,), (1,)), ((), ())), preferred_element_type=F32)


def pieces(a, count=3):
    parts = []
    for _ in range(count):
        part = a.astype(BF16).astype(F32)
        parts.append(part)
        a = a - part
    return parts


def stacked(a):
    return jnp.concatenate(pieces(a), axis=0).astype(BF16)


def stacked_small(a):
    parts = pieces(a)
    return jnp.concatenate(parts + [jnp.zeros_like(a)], axis=0).astype(BF16)


def unstack(a, rows):
    return a[:rows] + (a[rows : 2 * rows] + a[2 * rows : 3 * rows])


def iota(shape, axis):
    return lax.broadcasted_iota(jnp.int32, shape, axis)


def inverse_factors(grams, rank):
    count = range(len(grams))
    rest = list(grams)
    panels = [[] for _ in count]
    for base in range(0, rank, 8):
        rows = iota(rest[0].shape, 0)
        cols = [[jnp.broadcast_to(rest[m][:, base + j : base + j + 1], rest[m].shape) for j in range(8)] for m in count]
        scale = [jnp.zeros((8, LANES), F32) for _ in count]
        for j in range(8):
            for m in count:
                pivot = cols[m][j][j : j + 1]
                inverse = 1.0 / pivot
                scale[m] = jnp.where(rows[:8] == j, lax.rsqrt(pivot), scale[m])
                multiplier = jnp.where(rows > j, cols[m][j], 0.0)
                for other in range(j + 1, 8):
                    cols[m][other] = cols[m][other] - multiplier * (cols[m][other][j : j + 1] * inverse)
                rest[m] = rest[m] - multiplier * (rest[m][j : j + 1] * inverse)
        for m in count:
            panels[m].append(rest[m][:8] * scale[m])
            rest[m] = rest[m][8:]
    return [jnp.concatenate(panels[m], axis=0)[:, AUG : AUG + rank] for m in count]


def kernel(
    nt, ny, nz, factor,
    x_hbm, proj_hbm, gain_hbm, win_hbm, wout_hbm, og_hbm, ls_hbm, rs_hbm,
    emb, lbasis_ref, lupd_ref, rbasis_ref, rupd_ref,
    x, proj, gain_in, win, wout, og, ls, rs,
    wp, perm, dhid, hid, dpre, ls3, og_r3, pt, y_both, mixed_all,
    sib_send, sib_recv, feat_send, feat_recv, norm, norm_bf, dn_send, dn_recv, dfeat,
    t_send, t_recv, big_send, big1, big2_send, big2, raw, upd,
    small_send, small1, small2_send, small2, lraw, rupd,
    gram_all,
    local_sems, send_sems, recv_sems,
):
    rank, hidden = ls.shape
    rows = x.shape[0]
    examples = norm.shape[0]
    half = hidden // 2
    width = norm.shape[1]
    nx = nt // 2
    dp, t = lax.axis_index("dp"), lax.axis_index("tensor")
    y, z = dp // nz, dp % nz
    chip, core = t // 2, t % 2

    def others(me, n, device):
        offsets = sorted(range(1, n), key=lambda i: -min(i, n - i))
        return me, [(i, (me + i) % n, device((me + i) % n)) for i in offsets]

    groups = {
        "t": others(t, nt, lambda p: (dp, p)),
        "y": others(y, ny, lambda p: (p * nz + z, t)),
        "z": others(z, nz, lambda p: (y * nz + p, t)),
        "x": others(chip, nx, lambda p: (dp, 2 * p + core)),
        "c": others(core, 2, lambda p: (dp, 2 * chip + p)),
    }

    barrier = pltpu.get_barrier_semaphore()
    for axis in "tyz":
        for _, _, device in groups[axis][1]:
            pl.semaphore_signal(barrier, inc=1, device_id=device, device_id_type=MESH)

    def remote(stage, i, src, dst, sem, device):
        return pltpu.make_async_remote_copy(
            src_ref=src, dst_ref=dst, send_sem=send_sems.at[stage, i], recv_sem=recv_sems.at[stage, sem],
            device_id=device, device_id_type=MESH,
        )

    sent = []

    def send_one(stage, i, src, dst, sem, device):
        remote(stage, i, src, dst, sem, device).start()
        sent.append((stage, i, src, sem, device))

    def send(stage, axis, src, dst):
        me, peers = groups[axis]
        for i, p, device in peers:
            send_one(stage, i, src(p), dst(me), me, device)

    def receive(stage, axis, dst):
        for i, p, device in groups[axis][1]:
            remote(stage, i, dst(p), dst(p), p, device).wait_recv()

    def drain():
        for stage, i, src, sem, device in sent:
            remote(stage, i, src, src, sem, device).wait_send()
        sent.clear()

    loads = [
        pltpu.make_async_copy(a, b, local_sems.at[i])
        for i, (a, b) in enumerate(
            ((proj_hbm, proj), (x_hbm, x), (gain_hbm, gain_in), (win_hbm, win), (og_hbm, og), (rs_hbm, rs),
             (wout_hbm, wout), (ls_hbm, ls))
        )
    ]
    for load in loads:
        load.start()

    own = KF * GROUP
    slice_width = rows // examples
    block = GROUP * slice_width
    loads[0].wait()
    pick = (iota((own, KF), 0) // GROUP == iota((own, KF), 1)).astype(F32).astype(BF16)
    pt[...] = dot(pick, proj[...]).astype(BF16)

    loads[1].wait()
    y_t = dot_t(pt[...], x[...])
    keep = iota((own, rows), 0) % GROUP == (iota((own, rows), 1) // slice_width) % GROUP
    y_hi, y_lo = pieces(jnp.where(keep, y_t, 0.0), 2)
    y_both[:own, :] = y_hi.astype(BF16)
    y_both[own:, :] = y_lo.astype(BF16)

    def feature_part(g, target, slot):
        part = pl.ds(pl.multiple_of(g * block, block), block)
        both = dot(y_both[:, part], x[part, :])
        out = both[:own] + both[own:]
        for k in range(KF):
            target[slot, :, k * LANES : (k + 1) * LANES] = out[k * GROUP : (k + 1) * GROUP]

    for p in range(nx):
        feature_part(2 * p + 1 - core, sib_send, p)
    pl.semaphore_wait(barrier, sum(len(groups[axis][1]) for axis in "tyz"))
    send(FEAT_C, "c", lambda p: sib_send, lambda p: sib_recv)
    for p in range(nx):
        feature_part(2 * p + core, feat_send, p)
    receive(FEAT_C, "c", lambda p: sib_recv)
    for p in range(nx):
        feat_send[p] = feat_send[p] + sib_recv[p]
    send(FEAT, "x", lambda p: feat_send.at[p], lambda p: feat_recv.at[p])
    feat_recv[chip] = feat_send[chip]

    column = iota((width, width), 1)
    row = iota((width, width), 0)
    perm[...] = (column == (row % LANES) * KF + row // LANES).astype(F32).astype(BF16)
    loads[2].wait()
    gain_rows = jnp.concatenate(pieces(gain_in[...]) + [jnp.zeros((5, width), F32)], axis=0).astype(BF16)
    gain = dot_t(gain_rows, perm[...])
    gain = gain[0:1] + (gain[1:2] + gain[2:3])
    loads[3].wait()
    step = min(256, half)
    for c in range(0, hidden, step):
        wp[:, c : c + step] = dot(perm[...], win[:, c : c + step]).astype(BF16)
    loads[4].wait()
    loads[5].wait()
    og_r3[...] = stacked(unstack(dot_t(stacked(rs[...]), og[...]), rank) * factor)

    def eight(p):
        return pl.ds(pl.multiple_of(p * 8, 8), 8)

    def sixteen(p):
        return pl.ds(pl.multiple_of(p * GROUP, GROUP), GROUP)

    def total_of(ref, count):
        total = ref[0]
        for p in range(1, count):
            total = total + ref[p]
        return total

    receive(FEAT, "x", lambda p: feat_recv.at[p])
    features = total_of(feat_recv, nx)
    centered = features - jnp.sum(features, axis=1, keepdims=True) * (1.0 / width)
    rstd = lax.rsqrt(jnp.sum(centered * centered, axis=1, keepdims=True) * (1.0 / width) + 1e-05)
    xhat = centered * rstd
    mine = sixteen(t)
    norm[mine, :] = (xhat * gain).astype(BF16).astype(F32)

    def norm_of(p, c):
        return norm.at[sixteen(2 * p + c), :]

    send(NORM_X, "x", lambda p: norm_of(chip, core), lambda p: norm_of(p, core))
    send(NORM_C, "c", lambda p: norm_of(chip, core), lambda p: norm_of(chip, p))
    loads[6].wait()
    for c in range(0, hidden, step):
        dhid[:, c : c + step] = dot_t(og[...], wout[c : c + step, :])
    loads[7].wait()
    ls3[...] = stacked(ls[...])
    _, _, sibling = groups["c"][1][0]
    for i, p, device in reversed(groups["x"][1]):
        remote(NORM_X, i, norm_of(p, core), norm_of(p, core), p, device).wait_recv()
        send_one(NORM_F, i, norm_of(p, core), norm_of(p, core), p, sibling)
    receive(NORM_C, "c", lambda p: norm_of(chip, p))
    for i, p, device in reversed(groups["x"][1]):
        remote(NORM_F, i, norm_of(p, 1 - core), norm_of(p, 1 - core), p, sibling).wait_recv()
    norm_bf[...] = norm[...].astype(BF16)

    for c in range(0, hidden, step):
        cols = slice(c, c + step)
        pre = dot(norm_bf[...], wp[:, cols])
        sigma = jax.nn.sigmoid(pre)
        hid[:, cols] = (pre * sigma).astype(BF16)
        dpre[:, cols] = (dhid[:, cols] * sigma * (1.0 + pre * (1.0 - sigma))).astype(BF16)

    def factor_sum(stage, value):
        r = int(stage == V_SUM)
        t_send[r] = value
        dst = lambda p: t_recv.at[r, p]
        send(stage, "t", lambda p: t_send.at[r, eight(p), :], dst)
        t_recv[r, t] = t_send[r, eight(t), :]

        def finish():
            receive(stage, "t", dst)
            return total_of(t_recv.at[r], nt)

        return finish

    def big_first(r, h):
        stage, axis = ((A1_0, A1_1), (B1_0, B1_1))[r][h], "yz"[h]
        cols = pl.ds(h * half, half)
        dst = lambda p: big1.at[r, h, p]
        send(stage, axis, lambda p: big_send.at[r, eight(p), cols], dst)
        me = groups[axis][0]
        big1[r, h, me] = big_send[r, eight(me), h * half : (h + 1) * half]
        return lambda: receive(stage, axis, dst)

    def everywhere(stage, axis, value, source, slots, r, h):
        source[r, h] = value
        dst = lambda p: slots.at[r, h, p]
        send(stage, axis, lambda p: source.at[r, h], dst)
        slots[r, h, groups[axis][0]] = value
        return lambda: receive(stage, axis, dst)

    def big_second(r, h):
        stage = ((A2_0, A2_1), (B2_0, B2_1))[r][h]
        return everywhere(stage, "zy"[h], total_of(big1.at[r, h], (ny, nz)[h]), big2_send, big2, r, h)

    def big_third(r, h, target):
        stage, axis = ((A3_0, A3_1), (B3_0, B3_1))[r][h], "yz"[h]
        me = groups[axis][0]
        cols = pl.ds(h * half, half)
        target[eight(me), h * half : (h + 1) * half] = total_of(big2.at[r, h], (nz, ny)[h])
        dst = lambda p: target.at[eight(p), cols]
        send(stage, axis, lambda p: target.at[eight(me), cols], dst)
        return lambda: receive(stage, axis, dst)

    quarter = width // 2

    def small_first(r, h, value):
        stage = ((L1_0, L1_1), (S1_0, S1_1))[r][h]
        return everywhere(stage, "yz"[h], value, small_send, small1, r, h)

    def small_second(r, h):
        stage = ((L2_0, L2_1), (S2_0, S2_1))[r][h]
        return everywhere(stage, "zy"[h], total_of(small1.at[r, h], (ny, nz)[h]), small2_send, small2, r, h)

    def small_third(r, target):
        stage = (L3, S3)[r]
        for h in range(2):
            target[eight(t), h * quarter : (h + 1) * quarter] = total_of(small2.at[r, h], (nz, ny)[h])
        dst = lambda p: target.at[eight(p), :]
        send(stage, "t", lambda p: target.at[eight(t), :], dst)
        return lambda: receive(stage, "t", dst)

    t_done = factor_sum(T_SUM, unstack(dot_t(ls3[...], dpre[...]), rank) * factor)
    a1 = []
    for h in range(2):
        big_send[0, :, h * half : (h + 1) * half] = unstack(dot(og_r3[...], hid[:, h * half : (h + 1) * half]), rank)
        a1.append(big_first(0, h))
    d_partial = dot_t(dpre[...], wp[...])
    for g in range(nt):
        dn_send[g] = d_partial[g * GROUP : (g + 1) * GROUP]
    send(DNORM, "t", lambda p: dn_send.at[p], lambda p: dn_recv.at[p])
    dn_recv[t] = dn_send[t]

    pt_two = jnp.concatenate([pt[...]] * 2, axis=0)
    same = iota((block, 2 * own), 0) // slice_width == iota((block, 2 * own), 1) % GROUP
    for g in range(nt):
        part = slice(g * block, (g + 1) * block)
        mixed = jnp.where(same, dot_t(x[part, :], pt_two), 0.0)
        mixed_all[part, :] = jnp.concatenate(pieces(mixed, 2), axis=1).astype(BF16)

    left = unstack(dot(stacked_small(t_done()), norm_bf[...]), 8)
    l1 = [small_first(0, h, left[:, h * quarter : (h + 1) * quarter]) for h in range(2)]
    drain()

    a2 = []
    for h in range(2):
        a1[h]()
        a2.append(big_second(0, h))

    receive(DNORM, "t", lambda p: dn_recv.at[p])
    scaled = total_of(dn_recv, nt) * gain
    mean = jnp.sum(scaled, axis=1, keepdims=True) * (1.0 / width)
    slope = jnp.sum(scaled * xhat, axis=1, keepdims=True) * (1.0 / width)
    dfeat[mine, :] = (scaled - mean - xhat * slope) * rstd
    send(DFEAT, "t", lambda p: dfeat.at[mine, :], lambda p: dfeat.at[sixteen(p), :])

    l2 = []
    for h in range(2):
        l1[h]()
        l2.append(small_second(0, h))
    a3 = []
    for h in range(2):
        a2[h]()
        a3.append(big_third(0, h, raw))
    for h in range(2):
        l2[h]()
    l3 = small_third(0, lraw)

    receive(DFEAT, "t", lambda p: dfeat.at[sixteen(p), :])
    pt_all = jnp.concatenate([pt[...]] * 4, axis=0)
    for g in range(nt):
        part = slice(g * block, (g + 1) * block)
        d = dfeat[g * GROUP : (g + 1) * GROUP, :]
        d = jnp.concatenate([d[:, k * LANES : (k + 1) * LANES] for k in range(KF)], axis=0)
        d_two = jnp.concatenate(pieces(d, 2), axis=0).astype(BF16)
        through = jnp.where(same, dot_t(x[part, :], d_two), 0.0)
        through = jnp.concatenate(pieces(through, 2), axis=1).astype(BF16)
        both_sides = jnp.concatenate([through, mixed_all[part, :]], axis=1)
        emb[part, :] = dot(both_sides, jnp.concatenate([pt_all, d_two, d_two], axis=0)).astype(BF16)

    l3()
    u3 = stacked(unstack(dot_t(stacked(lraw[...]), norm_bf[...]), rank) * factor)
    b1 = []
    for h in range(2):
        big_send[1, :, h * half : (h + 1) * half] = unstack(dot(u3, dpre[:, h * half : (h + 1) * half]), rank)
        b1.append(big_first(1, h))

    for h in range(2):
        a3[h]()
    v_done = factor_sum(V_SUM, unstack(dot_t(stacked(raw[...]), hid[...]), rank) * factor)

    def gram_of(ref):
        gram = lax.dot_general(ref[...], ref[...], (((1,), (1,)), ((), ())), precision=HIGH, preferred_element_type=F32)
        return jnp.concatenate([gram, jnp.zeros((rank, LANES - rank), F32)], axis=1)

    gram_all[t] = gram_of(raw)
    send(GRAM, "t", lambda p: gram_all.at[t], lambda p: gram_all.at[p])
    unit = (iota((rank, LANES), 1) - AUG == iota((rank, LANES), 0)).astype(F32)
    left_gram = gram_of(lraw) + unit

    right = unstack(dot(stacked_small(v_done()), og[...]), 8)
    s1 = [small_first(1, h, right[:, h * quarter : (h + 1) * quarter]) for h in range(2)]
    drain()
    receive(GRAM, "t", lambda p: gram_all.at[p])
    right_gram = total_of(gram_all, nt) + unit
    b2 = []
    for h in range(2):
        b1[h]()
        b2.append(big_second(1, h))
    s2 = []
    for h in range(2):
        s1[h]()
        s2.append(small_second(1, h))

    left_inv, right_inv = inverse_factors([left_gram, right_gram], rank)

    b3 = []
    for h in range(2):
        b2[h]()
        b3.append(big_third(1, h, upd))
    for h in range(2):
        s2[h]()
    s3 = small_third(1, rupd)

    def high(a, b):
        return jnp.dot(a, b, precision=HIGH, preferred_element_type=F32)

    lbasis_ref[...] = unstack(dot(stacked(high(left_inv, lraw[...])), perm[...]), rank)
    rbasis_ref[...] = high(right_inv, raw[...])
    drain()
    for h in range(2):
        b3[h]()
    lupd_ref[...] = high(left_inv, upd[...])
    s3()
    rupd_ref[...] = high(right_inv, rupd[...])


def store_kernel(*refs):
    count = len(refs) // 2
    copies = [pltpu.make_async_copy(refs[i], refs[count + i], refs[-1].at[i]) for i in range(count)]
    for copy in copies:
        copy.start()
    for copy in copies:
        copy.wait()


def solution(mesh):
    nt = mesh.shape["tensor"]
    ny = nz = math.isqrt(mesh.shape["dp"])

    def on_device(embeddings, projection, gain, weight_in, weight_out, out_grad, left_start, right_start):
        examples, slice_width, emb_width = embeddings.shape
        rows = examples * slice_width
        width, hidden = weight_in.shape
        rank = left_start.shape[0]
        factor = 1.0 / math.sqrt(examples * ny * nz)
        half, quarter = hidden // 2, width // 2
        vmem = pl.BlockSpec(memory_space=pltpu.VMEM)
        hbm = pl.BlockSpec(memory_space=pltpu.HBM)
        n = max(ny, nz)
        out = pl.pallas_call(
            functools.partial(kernel, nt, ny, nz, factor),
            out_shape=(
                jax.ShapeDtypeStruct((rows, emb_width), BF16),
                jax.ShapeDtypeStruct((rank, width), F32),
                jax.ShapeDtypeStruct((rank, hidden), F32),
                jax.ShapeDtypeStruct((rank, hidden), F32),
                jax.ShapeDtypeStruct((rank, width), F32),
            ),
            in_specs=[hbm] * 8,
            out_specs=(vmem,) * 5,
            scratch_shapes=[
                pltpu.VMEM((rows, emb_width), BF16),
                pltpu.VMEM((projection.shape[1], emb_width), BF16),
                pltpu.VMEM((1, width), F32),
                pltpu.VMEM((width, hidden), BF16),
                pltpu.VMEM(weight_out.shape, BF16),
                pltpu.VMEM(out_grad.shape, BF16),
                pltpu.VMEM((rank, hidden), F32),
                pltpu.VMEM(right_start.shape, F32),
                pltpu.VMEM((width, hidden), BF16),
                pltpu.VMEM((width, width), BF16),
                pltpu.VMEM((examples, hidden), F32),
                pltpu.VMEM((examples, hidden), BF16),
                pltpu.VMEM((examples, hidden), BF16),
                pltpu.VMEM((3 * rank, hidden), BF16),
                pltpu.VMEM((3 * rank, examples), BF16),
                pltpu.VMEM((KF * GROUP, emb_width), BF16),
                pltpu.VMEM((2 * KF * GROUP, rows), BF16),
                pltpu.VMEM((rows, 4 * KF * GROUP), BF16),
                pltpu.VMEM((nt // 2, GROUP, width), F32),
                pltpu.VMEM((nt // 2, GROUP, width), F32),
                pltpu.VMEM((nt // 2, GROUP, width), F32),
                pltpu.VMEM((nt // 2, GROUP, width), F32),
                pltpu.VMEM((examples, width), F32),
                pltpu.VMEM((examples, width), BF16),
                pltpu.VMEM((nt, GROUP, width), F32),
                pltpu.VMEM((nt, GROUP, width), F32),
                pltpu.VMEM((examples, width), F32),
                pltpu.VMEM((2, rank, examples), F32),
                pltpu.VMEM((2, nt, 8, examples), F32),
                pltpu.VMEM((2, rank, hidden), F32),
                pltpu.VMEM((2, 2, n, 8, half), F32),
                pltpu.VMEM((2, 2, 8, half), F32),
                pltpu.VMEM((2, 2, n, 8, half), F32),
                pltpu.VMEM((rank, hidden), F32),
                pltpu.VMEM((rank, hidden), F32),
                pltpu.VMEM((2, 2, 8, quarter), F32),
                pltpu.VMEM((2, 2, n, 8, quarter), F32),
                pltpu.VMEM((2, 2, 8, quarter), F32),
                pltpu.VMEM((2, 2, n, 8, quarter), F32),
                pltpu.VMEM((rank, width), F32),
                pltpu.VMEM((rank, width), F32),
                pltpu.VMEM((nt, rank, LANES), F32),
                pltpu.SemaphoreType.DMA((8,)),
                pltpu.SemaphoreType.DMA((STAGES, max(n, nt))),
                pltpu.SemaphoreType.DMA((STAGES, max(n, nt))),
            ],
            compiler_params=pltpu.CompilerParams(
                collective_id=0, has_side_effects=True, vmem_limit_bytes=48 * 1024 * 1024
            ),
            name="fused_backward",
        )(
            *(
                pltpu.with_memory_space_constraint(a, pltpu.HBM)
                for a in (
                    embeddings.reshape(rows, emb_width), projection.T, gain.reshape(1, width),
                    weight_in, weight_out, out_grad, left_start, right_start,
                )
            )
        )
        out = pl.pallas_call(
            store_kernel,
            out_shape=[jax.ShapeDtypeStruct(a.shape, a.dtype) for a in out],
            in_specs=[vmem] * 5,
            out_specs=[hbm] * 5,
            scratch_shapes=[pltpu.SemaphoreType.DMA((5,))],
            name="store",
        )(*out)
        return (out[0].reshape(embeddings.shape), *out[1:])

    return jax.shard_map(
        on_device,
        mesh=mesh,
        in_specs=(
            P("dp", "tensor", None),
            P(),
            P(),
            P(None, "tensor"),
            P("tensor", None),
            P("dp", None),
            P(None, "tensor"),
            P(),
        ),
        out_specs=(P("dp", "tensor", None), P(), P(None, "tensor"), P(None, "tensor"), P()),
        check_vma=False,
    )
```
